256 devices in a mesh: dp: 8 (over x_lo, y), fsdp: 32 (over x_hi, z, core).
Axes of the slice: x: 4 (x_hi: 2, x_lo: 2; x = x_hi * 2 + x_lo), y: 4, z: 8, core: 2. Of those that a mesh axis runs over, the one named last changes fastest.
Arguments:
- layer_input: bfloat16 [65536, 8192], P(('dp', 'fsdp')), may hold values from -6 to 6
- value_grad: bfloat16 [65536, 1024], P(('dp', 'fsdp')), may hold values from -6 to 6
- base_weight_t: bfloat16 [1024, 8192], P('fsdp'), may hold values from -0.1875 to 0.1875
- adapter_down: bfloat16 [8192, 64], replicated, may hold values from -0.0625 to 0.0625
- adapter_up: bfloat16 [64, 1024], replicated, may hold values from -0.75 to 0.75
Outputs:
- input_gradient: bfloat16 [65536, 8192], P(('dp', 'fsdp'))
- down_grad: float32 [8192, 64], replicated
- up_grad: float32 [64, 1024], replicated
The draws below stay inside these ranges and needn't reach their ends.
All inputs are finite; a program needn't handle non-finite values.
Results may differ from the reference program's by a relative error of at most 0.0034.
Values may be sent and summed in bfloat16 or wider, within the bound.
No kernel may reach another device: no remote copies, remote signals or barrier semaphores. Data moves between devices by JAX's collectives and lax.ppermute only.
A program may use at most 128 MiB of HBM per device.

```python
import jax
import jax.numpy as jnp
from jax import lax

D = 8192
KV = 1024
R = 64
TOKEN_TOTAL = 65536
N_DP = 8


def steps_of(rng, dims, split, low, high):
    gain = 1.0
    for axis_at, parts in split:
        steps = jax.random.uniform(jax.random.fold_in(jax.random.fold_in(rng, 6), axis_at), (parts,), jnp.float32, low / len(split), high / len(split))
        gain = gain * jnp.repeat(jnp.exp(steps), dims[axis_at] // parts).reshape((-1,) + (1,) * (len(dims) - 1 - axis_at))
    return gain


def scatter_about(key, dims, width, limit, shards=(), kind=jnp.bfloat16):
    drawn = width * jax.random.normal(key, dims, jnp.float32)
    if shards:
        drawn = drawn * steps_of(key, dims, shards, -0.22, 0.18)
    return jnp.clip(drawn, -limit, limit).astype(kind)


def setup_inputs(seed: int = 0) -> dict:
    seeds = jax.random.split(jax.random.key(seed), 6)
    layer_input = scatter_about(seeds[0], (TOKEN_TOTAL, D), 1.0, 6.0, ((0, 256),))
    value_grad = scatter_about(seeds[1], (TOKEN_TOTAL, KV), 1.0, 6.0, ((0, 256),))
    base_weight_t = scatter_about(seeds[2], (KV, D), KV ** -0.5, 0.1875, ((0, 32),))
    adapter_down = scatter_about(seeds[3], (D, R), D ** -0.5, 0.0625)
    adapter_up = scatter_about(seeds[4], (R, KV), R ** -0.5, 0.75)
    return {"layer_input": layer_input, "value_grad": value_grad, "base_weight_t": base_weight_t, "adapter_down": adapter_down, "adapter_up": adapter_up}


adapter_scale = 2.0

def reference(layer_input, value_grad, base_weight_t, adapter_down, adapter_up):
    projected = jnp.dot(layer_input, adapter_down, preferred_element_type=jnp.float32).astype(jnp.bfloat16)
    pulled = jnp.dot(value_grad, adapter_up.T, preferred_element_type=jnp.float32).astype(jnp.bfloat16)
    adapter_factor = adapter_scale / jnp.sqrt(jnp.float32(TOKEN_TOTAL))
    up_grad = adapter_factor * jnp.dot(projected.T, value_grad, preferred_element_type=jnp.float32)
    down_grad = adapter_factor * jnp.dot(layer_input.T, pulled, preferred_element_type=jnp.float32)
    grad_blocks = value_grad.reshape(N_DP, TOKEN_TOTAL // N_DP, KV)
    pulled_blocks = pulled.reshape(N_DP, TOKEN_TOTAL // N_DP, R)

    def one_block(pair):
        grad_rows, pulled_rows = pair
        frozen_weight = jnp.dot(grad_rows, base_weight_t, preferred_element_type=jnp.float32)
        adapter_extra = jnp.dot(pulled_rows, adapter_down.T, preferred_element_type=jnp.float32)
        return (frozen_weight + adapter_scale * adapter_extra).astype(jnp.bfloat16)
    input_gradient = lax.map(one_block, (grad_blocks, pulled_blocks)).reshape(TOKEN_TOTAL, D)
    return (input_gradient, down_grad, up_grad)
```

```python
import functools
import math

import jax
import jax.numpy as jnp
from jax import lax
from jax.experimental import pallas as pl
from jax.experimental.pallas import tpu as pltpu
from jax.sharding import Mesh
from jax.sharding import PartitionSpec as P

adapter_scale = 2.0
AXES = ("x_lo", "y", "x_hi", "z", "core")
SIZES = (2, 4, 2, 8, 2)
HALF = 4096
ZCOLS = 2560
YQ = 384
f32, bf16 = jnp.float32, jnp.bfloat16


def shift(x, axis, k):
    n = SIZES[AXES.index(axis)]
    return lax.ppermute(x, axis, [(i, (i + k) % n) for i in range(n)])


def flip(x, axis, k):
    n = SIZES[AXES.index(axis)]
    return lax.ppermute(x, axis, [(i, i ^ k) for i in range(n)])


def shift_x(x, k):
    place = lambda at: (at % 2) * 2 + at // 2
    return lax.ppermute(x, ("x_lo", "x_hi"), [(place(i), place((i + k) % 4)) for i in range(4)])


def cross_x(x):
    return lax.ppermute(x, ("x_lo", "x_hi"), [(0, 3), (3, 0), (1, 2), (2, 1)])


def product_kernel(x_ref, w_ref, p_ref, d_ref, own_ref, other_ref):
    total = jnp.dot(x_ref[...], w_ref[...], preferred_element_type=f32)
    total += lax.dot_general(
        p_ref[...], d_ref[...], (((1,), (1,)), ((), ())), preferred_element_type=f32
    )
    total = total.astype(bf16)
    rows = own_ref.shape[0]
    own_ref[...] = total[:rows]
    other_ref[...] = total[rows:]


def product(x, w, p, d, step):
    tokens, depth = x.shape
    n = d.shape[0]
    if w.ndim == 2:
        w_spec = pl.BlockSpec((depth, step), lambda i: (0, i))
    else:
        w_spec = pl.BlockSpec((None, depth, step), lambda i: (i, 0, 0))
    out = jax.ShapeDtypeStruct((tokens // 2, n), bf16)
    out_spec = pl.BlockSpec((tokens // 2, step), lambda i: (0, i))
    return pl.pallas_call(
        product_kernel,
        grid=(n // step,),
        in_specs=[
            pl.BlockSpec((tokens, depth), lambda i: (0, 0)),
            w_spec,
            pl.BlockSpec((tokens, p.shape[1]), lambda i: (0, 0)),
            pl.BlockSpec((step, d.shape[1]), lambda i: (i, 0)),
        ],
        out_specs=[out_spec, out_spec],
        out_shape=[out, out],
        compiler_params=pltpu.CompilerParams(vmem_limit_bytes=32 * 2**20),
        cost_estimate=pl.CostEstimate(
            flops=2 * tokens * depth * n, bytes_accessed=2 * depth * n + 2 * tokens * n, transcendentals=0
        ),
    )(x, w, p, d)


def adapter_kernel(li_ref, down_ref, vg_ref, pulled_ref, down_part_ref, up_part_ref, proj, *, factor):
    i = pl.program_id(0)

    @pl.when(i == 0)
    def _():
        proj[...] = jnp.zeros_like(proj)

    li = li_ref[...]
    proj[...] += jnp.dot(li, down_ref[...], preferred_element_type=f32)
    down_part_ref[...] = factor * lax.dot_general(
        pulled_ref[...], li, (((0,), (0,)), ((), ())), preferred_element_type=f32
    )

    @pl.when(i == pl.num_programs(0) - 1)
    def _():
        up_part_ref[...] = factor * lax.dot_general(
            proj[...].astype(bf16), vg_ref[...], (((0,), (0,)), ((), ())), preferred_element_type=f32
        )


def adapter_parts(li, down, vg, pulled, factor, step=1024):
    tokens, width = li.shape
    rank = down.shape[1]
    features = vg.shape[1]
    return pl.pallas_call(
        functools.partial(adapter_kernel, factor=factor),
        grid=(width // step,),
        in_specs=[
            pl.BlockSpec((tokens, step), lambda i: (0, i)),
            pl.BlockSpec((step, rank), lambda i: (i, 0)),
            pl.BlockSpec((tokens, features), lambda i: (0, 0)),
            pl.BlockSpec((tokens, rank), lambda i: (0, 0)),
        ],
        out_specs=[
            pl.BlockSpec((rank, step), lambda i: (0, i)),
            pl.BlockSpec((rank, features), lambda i: (0, 0)),
        ],
        out_shape=[
            jax.ShapeDtypeStruct((rank, width), f32),
            jax.ShapeDtypeStruct((rank, features), f32),
        ],
        scratch_shapes=[pltpu.VMEM((tokens, rank), f32)],
        compiler_params=pltpu.CompilerParams(vmem_limit_bytes=32 * 2**20),
        cost_estimate=pl.CostEstimate(
            flops=4 * tokens * width * rank, bytes_accessed=2 * tokens * width + 4 * rank * width, transcendentals=0
        ),
    )(li, down, vg, pulled)


def pair(first_is_mine, mine, other):
    return jnp.where(first_is_mine, jnp.stack([mine, other]), jnp.stack([other, mine]))


def local(layer_input, value_grad, base_weight_t, adapter_down, adapter_up):
    core, y, z = lax.axis_index("core"), lax.axis_index("y"), lax.axis_index("z")
    x_hi = lax.axis_index("x_hi")
    x = 2 * x_hi + lax.axis_index("x_lo")
    tokens = value_grad.shape[0]
    factor = adapter_scale / math.sqrt(tokens * math.prod(SIZES))
    rank, features = adapter_up.shape

    mine = lax.dynamic_slice_in_dim(base_weight_t, core * HALF, HALF, 1)
    give = lax.dynamic_slice_in_dim(base_weight_t, (1 - core) * HALF, HALF, 1)
    chip_rows = pair(core == 0, mine, flip(give, "core", 1)).reshape(-1, HALF)

    quarter = lax.dynamic_slice_in_dim(chip_rows, ZCOLS + YQ * y, YQ, 1)
    line = lax.all_gather(quarter, "z", axis=0, tiled=True)
    both = pair(x_hi == 0, line, cross_x(line)).reshape(-1, YQ)
    weight_y = lax.all_gather(both, "y", axis=0, tiled=False)

    strip = chip_rows[:, :ZCOLS]
    strips = pair(x_hi == 0, strip, cross_x(strip)).reshape(-1, ZCOLS)
    weight_z = lax.all_gather(strips, "z", axis=0, tiled=True)

    pulled = lax.dot_general(
        value_grad, adapter_up, (((1,), (1,)), ((), ())), preferred_element_type=f32
    ).astype(bf16)
    down_part, up_part = adapter_parts(layer_input, adapter_down, value_grad, pulled, factor)

    half_up = features // 2
    halves = jnp.stack(
        [
            jnp.concatenate([down_part[:, :HALF], up_part[:, :half_up]], 1),
            jnp.concatenate([down_part[:, HALF:], up_part[:, half_up:]], 1),
        ]
    )
    keep = lax.dynamic_index_in_dim(halves, core, 0, False)
    total = keep + flip(lax.dynamic_index_in_dim(halves, 1 - core, 0, False), "core", 1)
    piece = total.shape[1] // 4
    part = lambda k: lax.dynamic_slice_in_dim(total, ((y + k) % 4) * piece, piece, 1)
    total_y = part(0) + shift(part(1), "y", 1) + shift(part(2), "y", 2) + shift(part(3), "y", 3)
    rows = rank // 4
    part_x = lambda k: lax.dynamic_slice_in_dim(total_y, ((x + k) % 4) * rows, rows, 0)
    total_x = part_x(0) + shift_x(part_x(1), 1) + shift_x(part_x(2), 2) + shift_x(part_x(3), 3)
    for k in (1, 2, 4):
        total_x = total_x + flip(total_x, "z", k)
    got = [total_x] + [shift_x(total_x, k) for k in (1, 2, 3)]
    line_x = jnp.zeros((rank, piece), f32)
    for k in range(4):
        line_x = lax.dynamic_update_slice_in_dim(line_x, got[k], ((x - k) % 4) * rows, 0)
    got = [line_x] + [shift(line_x, "y", k) for k in (1, 2, 3)]
    half = jnp.zeros((rank, piece * 4), f32)
    for k in range(4):
        half = lax.dynamic_update_slice_in_dim(half, got[k], ((y - k) % 4) * piece, 1)
    whole = pair(core == 0, half, flip(half, "core", 1))
    down_grad = jnp.concatenate([whole[0, :, :HALF], whole[1, :, :HALF]], 1).T
    up_grad = jnp.concatenate([whole[0, :, HALF:], whole[1, :, HALF:]], 1)

    grads = jnp.concatenate([value_grad, flip(value_grad, "core", 1)], 0)
    pulled_both = lax.dot_general(
        grads, adapter_up, (((1,), (1,)), ((), ())), preferred_element_type=f32
    ).astype(bf16)
    pulled_both = (adapter_scale * pulled_both).astype(bf16)
    down_half = lax.dynamic_slice_in_dim(adapter_down, core * HALF, HALF, 0)
    grads_z = grads.reshape(2 * tokens, 2, 8, -1).transpose(0, 2, 1, 3).reshape(2 * tokens, -1)
    own_z, other_z = product(grads_z, weight_z, pulled_both, down_half[:ZCOLS], 512)
    own_y, other_y = product(grads, weight_y, pulled_both, down_half[ZCOLS:], YQ)
    got_z, got_y = flip(other_z, "core", 1), flip(other_y, "core", 1)
    first = [jnp.where(core == 0, a, b) for a, b in ((own_z, got_z), (own_y, got_y))]
    second = [jnp.where(core == 0, b, a) for a, b in ((own_z, got_z), (own_y, got_y))]
    input_gradient = jnp.concatenate(first + second, 1)
    return (input_gradient, down_grad, up_grad)


def solution(mesh):
    fine = Mesh(mesh.devices.reshape(SIZES), AXES)
    return jax.shard_map(
        local,
        mesh=fine,
        in_specs=(P(AXES, None), P(AXES, None), P(("x_hi", "z", "core"), None), P(), P()),
        out_specs=(P(AXES, None), P(), P()),
        check_vma=False,
    )
```

```python
import functools
import math

import jax
import jax.numpy as jnp
from jax import lax
from jax.experimental import pallas as pl
from jax.experimental.pallas import tpu as pltpu
from jax.sharding import Mesh
from jax.sharding import PartitionSpec as P

adapter_scale = 2.0
AXES = ("x_lo", "y", "x_hi", "z", "core")
SIZES = (2, 4, 2, 8, 2)
D = 8192
HALF = D // 2
UCOLS = 2048
ZCOLS = HALF - UCOLS
STEP = 512
f32, bf16 = jnp.float32, jnp.bfloat16
ANY = pl.BlockSpec(memory_space=pl.ANY)


def shift(x, axis, k):
    n = SIZES[AXES.index(axis)]
    return lax.ppermute(x, axis, [(i, (i + k) % n) for i in range(n)])


def flip(x, axis, k):
    n = SIZES[AXES.index(axis)]
    return lax.ppermute(x, axis, [(i, i ^ k) for i in range(n)])


def cross_x(x):
    return lax.ppermute(x, ("x_lo", "x_hi"), [(0, 3), (3, 0), (1, 2), (2, 1)])


def after(x, *others):
    return lax.optimization_barrier((x, *others))[0]


def params(mib=32):
    return pltpu.CompilerParams(vmem_limit_bytes=mib * 2**20)


def product_kernel(at_ref, grads, pulled, down, *refs, paired):
    own_ref, other_ref = refs[-2:]
    half, step = grads.shape[1] // 2, own_ref.shape[1]
    total = jnp.dot(pulled[...], down[...], preferred_element_type=f32)
    for far in (0, 1):
        at = pl.ds(pl.multiple_of((at_ref[1] + far) % 2 * half, 128), half)
        rows = refs[0][:, far].reshape(half, step) if paired else refs[far][...]
        total += jnp.dot(grads[:, at], rows, preferred_element_type=f32)
    total = total.astype(bf16)
    rows = own_ref.shape[0]
    own_ref[...] = total[:rows]
    other_ref[...] = total[rows:]


def product(at, x_hi, grads, pulled, down_t, weights, result=None):
    tokens, n = grads.shape[0], weights[0].shape[-1]
    whole = lambda a: pl.BlockSpec(a.shape, lambda i, at: (0,) * a.ndim)
    args = [grads, pulled, down_t, *weights] + ([] if result is None else [result])
    weight_spec = lambda w: pl.BlockSpec((*w.shape[:-1], STEP), lambda i, at: (0,) * (w.ndim - 1) + (i,))
    size = sum(w.size for w in weights)
    return pl.pallas_call(
        functools.partial(product_kernel, paired=len(weights) == 1),
        grid_spec=pltpu.PrefetchScalarGridSpec(
            num_scalar_prefetch=1,
            grid=(n // STEP,),
            in_specs=[
                whole(grads),
                whole(pulled),
                pl.BlockSpec((pulled.shape[1], STEP), lambda i, at: (0, at[0] + i)),
            ]
            + [weight_spec(w) for w in weights]
            + ([] if result is None else [ANY]),
            out_specs=[
                pl.BlockSpec((tokens // 2, STEP), lambda i, at: (0, at[0] + i)),
                pl.BlockSpec((tokens // 2, STEP), lambda i, at: (0, i)),
            ],
        ),
        out_shape=[
            jax.ShapeDtypeStruct((tokens // 2, D), bf16),
            jax.ShapeDtypeStruct((tokens // 2, n), bf16),
        ],
        input_output_aliases={} if result is None else {len(args): 0},
        compiler_params=params(56),
        cost_estimate=pl.CostEstimate(
            flops=2 * tokens * size, bytes_accessed=2 * size + 2 * tokens * n, transcendentals=0
        ),
    )(jnp.stack([at // STEP, x_hi]), *args)


def place_kernel(at_ref, piece, _, out, sems, *, parts):
    step = piece.shape[1] // parts
    copies = []
    for k in range(parts):
        there = pl.ds(pl.multiple_of(at_ref[k], 128), step)
        source = piece.at[:, k * step : (k + 1) * step]
        copies.append(pltpu.make_async_copy(source, out.at[:, there], sems.at[k]))
    for copy in copies:
        copy.start()
    for copy in copies:
        copy.wait()


def place(at, piece, result):
    parts = at.shape[0]
    return pl.pallas_call(
        functools.partial(place_kernel, parts=parts),
        grid_spec=pltpu.PrefetchScalarGridSpec(
            num_scalar_prefetch=1,
            grid=(1,),
            in_specs=[pl.BlockSpec(piece.shape, lambda i, at: (0, 0)), ANY],
            out_specs=ANY,
            scratch_shapes=[pltpu.SemaphoreType.DMA((parts,))],
        ),
        out_shape=jax.ShapeDtypeStruct(result.shape, result.dtype),
        input_output_aliases={2: 0},
        compiler_params=params(),
        cost_estimate=pl.CostEstimate(flops=0, bytes_accessed=4 * piece.size, transcendentals=0),
    )(at, piece, result)


def adapter_kernel(core_ref, li_ref, down_ref, vg_ref, up_ref, keep_ref, give_ref, proj, pulled, *, factor):
    i = pl.program_id(0)
    step = li_ref.shape[1]
    rows = keep_ref.shape[1]
    blocks = pulled.shape[1] // rows
    per = keep_ref.shape[0] // blocks

    @pl.when(i == 0)
    def _():
        proj[...] = jnp.zeros_like(proj)
        pulled[...] = lax.dot_general(
            vg_ref[...], up_ref[...], (((1,), (1,)), ((), ())), preferred_element_type=f32
        ).astype(bf16)

    li = li_ref[...]
    proj[...] += lax.dot_general(
        li, down_ref[...], (((1,), (1,)), ((), ())), preferred_element_type=f32
    )
    part = factor * lax.dot_general(
        pulled[...], li, (((0,), (0,)), ((), ())), preferred_element_type=f32
    )
    mine = i // per == core_ref[0]

    def put(ref):
        for b in range(blocks):
            ref[b * per + i % per, :, :step] = part[b * rows : (b + 1) * rows]

    pl.when(mine)(lambda: put(keep_ref))
    pl.when(jnp.logical_not(mine))(lambda: put(give_ref))

    @pl.when(i == pl.num_programs(0) - 1)
    def _():
        up = factor * lax.dot_general(
            proj[...].astype(bf16), vg_ref[...], (((0,), (0,)), ((), ())), preferred_element_type=f32
        )
        h = up.shape[1] // 2
        w = h // per
        first = core_ref[0] == 0
        mine = jnp.where(first, up[:, :h], up[:, h:])
        other = jnp.where(first, up[:, h:], up[:, :h])
        for b in range(blocks):
            for c in range(per):
                part = slice(b * rows, (b + 1) * rows), slice(c * w, (c + 1) * w)
                keep_ref[b * per + c, :, step:] = mine[part]
                give_ref[b * per + c, :, step:] = other[part]


def adapter_parts(core, li, down_t, vg, up, factor, blocks=4, step=1024):
    tokens, width = li.shape
    rank, features = up.shape
    per = width // step // 2
    out = jax.ShapeDtypeStruct((blocks * per, rank // blocks, step + features // 2 // per), f32)
    whole = lambda a: pl.BlockSpec(a.shape, lambda i, c: (0,) * len(a.shape))
    return pl.pallas_call(
        functools.partial(adapter_kernel, factor=factor),
        grid_spec=pltpu.PrefetchScalarGridSpec(
            num_scalar_prefetch=1,
            grid=(width // step,),
            in_specs=[
                pl.BlockSpec((tokens, step), lambda i, c: (0, i)),
                pl.BlockSpec((rank, step), lambda i, c: (0, i)),
                whole(vg),
                whole(up),
            ],
            out_specs=[whole(out), whole(out)],
            scratch_shapes=[pltpu.VMEM((tokens, rank), f32), pltpu.VMEM((tokens, rank), bf16)],
        ),
        out_shape=[out, out],
        compiler_params=params(),
        cost_estimate=pl.CostEstimate(
            flops=4 * tokens * width * rank, bytes_accessed=2 * tokens * width + 4 * rank * width, transcendentals=0
        ),
    )(core, li, down_t, vg, up)


def finish_kernel(core_ref, mine, other, down_ref, up_ref, *, blocks):
    i = pl.program_id(0)
    step = down_ref.shape[1]
    per = mine.shape[0] // blocks

    def put(ref):
        for b in range(blocks):
            block = ref[b * per + i % per]
            rows = block.shape[0]
            down_ref[b * rows : (b + 1) * rows, :] = block[:, :step]
            up_ref[b * rows : (b + 1) * rows, :] = block[:, step:]

    pl.when(i < per)(lambda: put(mine))
    pl.when(i >= per)(lambda: put(other))


def finish(core, mine, other, rank, features, blocks=4, step=1024):
    per = mine.shape[0] // blocks
    whole = lambda a: pl.BlockSpec(a.shape, lambda i, c: (0,) * len(a.shape))
    at = lambda i, c: jnp.where(i < per, c[0], 1 - c[0]) * per + i % per
    return pl.pallas_call(
        functools.partial(finish_kernel, blocks=blocks),
        grid_spec=pltpu.PrefetchScalarGridSpec(
            num_scalar_prefetch=1,
            grid=(2 * per,),
            in_specs=[whole(mine), whole(other)],
            out_specs=[
                pl.BlockSpec((rank, step), lambda i, c: (0, at(i, c))),
                pl.BlockSpec((rank, features // 2 // per), lambda i, c: (0, at(i, c))),
            ],
        ),
        out_shape=[
            jax.ShapeDtypeStruct((rank, 2 * per * step), f32),
            jax.ShapeDtypeStruct((rank, features), f32),
        ],
        compiler_params=params(),
        cost_estimate=pl.CostEstimate(flops=0, bytes_accessed=8 * mine.size, transcendentals=0),
    )(core, mine, other)


def local(layer_input, value_grad, base_weight_t, adapter_down, adapter_up):
    core, x_hi = lax.axis_index("core"), lax.axis_index("x_hi")
    plane = ("x_lo", "y", "x_hi")
    tokens, features = value_grad.shape
    rank = adapter_up.shape[0]
    factor = adapter_scale / math.sqrt(tokens * math.prod(SIZES))
    down_t = adapter_down.T

    mine = lax.dynamic_slice_in_dim(base_weight_t, core * HALF, HALF, 1)
    give = lax.dynamic_slice_in_dim(base_weight_t, (1 - core) * HALF, HALF, 1)
    got = flip(give, "core", 1)
    chip_rows = jnp.where(core == 0, jnp.concatenate([mine, got]), jnp.concatenate([got, mine]))

    keep, give = adapter_parts(
        core.reshape(1), after(layer_input, chip_rows), down_t, value_grad, adapter_up, factor
    )
    total = keep + flip(give, "core", 1)
    total = lax.all_to_all(total, plane, 0, 0, tiled=True).sum(0)
    near = lax.all_gather(chip_rows[:, ZCOLS:], "z", axis=0, tiled=True)
    far = cross_x(after(near, total))
    strip = chip_rows[:, :ZCOLS]
    strips = after(jnp.stack([strip, cross_x(strip)]), near, total)
    weight_z = lax.all_gather(strips, "z", axis=0, tiled=False)

    for k in (1, 2, 4):
        total = total + flip(total, "z", k)
    half = lax.all_to_all(
        jnp.broadcast_to(total, (16, *total.shape)), plane, 0, 0, tiled=True
    )
    down_grad_t, up_grad = finish(core.reshape(1), half, flip(half, "core", 1), rank, features)

    grads = jnp.concatenate([value_grad, flip(value_grad, "core", 1)], 0)
    pulled = lax.dot_general(
        grads, adapter_up, (((1,), (1,)), ((), ())), preferred_element_type=f32
    ).astype(bf16)
    pulled = (adapter_scale * pulled).astype(bf16)
    result, send_u = product(core * HALF + ZCOLS, x_hi, grads, pulled, down_t, [near, far])
    result, send_z = product(core * HALF, x_hi, grads, pulled, down_t, [weight_z], result)
    base = (1 - core) * HALF
    result = place((base + ZCOLS).reshape(1), flip(send_u, "core", 1), result)
    result = place(base.reshape(1), flip(send_z, "core", 1), result)
    return (result, down_grad_t.T, up_grad)


def solution(mesh):
    fine = Mesh(mesh.devices.reshape(SIZES), AXES)
    return jax.shard_map(
        local,
        mesh=fine,
        in_specs=(P(AXES, None), P(AXES, None), P(("x_hi", "z", "core"), None), P(), P()),
        out_specs=(P(AXES, None), P(), P()),
        check_vma=False,
    )
```

```python
import functools
import math

import jax
import jax.numpy as jnp
from jax import lax
from jax.experimental import pallas as pl
from jax.experimental.pallas import tpu as pltpu
from jax.sharding import Mesh
from jax.sharding import PartitionSpec as P

adapter_scale = 2.0
AXES = ("x_lo", "y", "x_hi", "z", "core")
SIZES = (2, 4, 2, 8, 2)
D = 8192
HALF = D // 2
UCOLS = 2048
ZCOLS = HALF - UCOLS
f32, bf16 = jnp.float32, jnp.bfloat16
ANY = pl.BlockSpec(memory_space=pl.ANY)


def shift(x, axis, k):
    n = SIZES[AXES.index(axis)]
    return lax.ppermute(x, axis, [(i, (i + k) % n) for i in range(n)])


def flip(x, axis, k):
    n = SIZES[AXES.index(axis)]
    return lax.ppermute(x, axis, [(i, i ^ k) for i in range(n)])


def cross_x(x):
    return lax.ppermute(x, ("x_lo", "x_hi"), [(0, 3), (3, 0), (1, 2), (2, 1)])


def after(x, *others):
    return lax.optimization_barrier((x, *others))[0]


def params(mib=32):
    return pltpu.CompilerParams(vmem_limit_bytes=mib * 2**20)


def product_kernel(at_ref, grads, pulled, down, *refs, paired):
    own_ref, other_ref = refs[-2:]
    half, step = grads.shape[1] // 2, own_ref.shape[1]
    total = jnp.dot(pulled[...], down[...], preferred_element_type=f32)
    for far in (0, 1):
        at = pl.ds(pl.multiple_of((at_ref[1] + far) % 2 * half, 128), half)
        rows = refs[0][:, far].reshape(half, step) if paired else refs[far][...]
        total += jnp.dot(grads[:, at], rows, preferred_element_type=f32)
    total = total.astype(bf16)
    rows = own_ref.shape[0]
    own_ref[...] = total[:rows]
    other_ref[...] = total[rows:]


def product(ids, off, grads, pulled, down_t, weights, result=None, first=0, step=512):
    tokens, n = grads.shape[0], weights[-1].shape[-1]
    whole = lambda a: pl.BlockSpec(a.shape, lambda i, at: (0,) * a.ndim)
    args = [grads, pulled, down_t, *weights] + ([] if result is None else [result])
    block = lambda i, ids: (0, ids[0] * (HALF // step) + off // step + i)
    weight_spec = lambda w: pl.BlockSpec(
        (*w.shape[:-1], step), lambda i, at: (0,) * (w.ndim - 1) + (i + (first // step if w.shape[-1] > n else 0),)
    )
    return pl.pallas_call(
        functools.partial(product_kernel, paired=len(weights) == 1),
        grid_spec=pltpu.PrefetchScalarGridSpec(
            num_scalar_prefetch=1,
            grid=(n // step,),
            in_specs=[
                whole(grads),
                whole(pulled),
                pl.BlockSpec((pulled.shape[1], step), block),
            ]
            + [weight_spec(w) for w in weights]
            + ([] if result is None else [ANY]),
            out_specs=[
                pl.BlockSpec((tokens // 2, step), block),
                pl.BlockSpec((tokens // 2, step), lambda i, at: (0, i)),
            ],
        ),
        out_shape=[
            jax.ShapeDtypeStruct((tokens // 2, D), bf16),
            jax.ShapeDtypeStruct((tokens // 2, n), bf16),
        ],
        input_output_aliases={} if result is None else {len(args): 0},
        compiler_params=params(56),
        cost_estimate=pl.CostEstimate(flops=0, bytes_accessed=0, transcendentals=0),
    )(ids, *args)


def place_kernel(ids_ref, piece, _, out, sem, *, off):
    there = pl.multiple_of((1 - ids_ref[0]) * HALF + off, 128)
    copy = pltpu.make_async_copy(piece, out.at[:, pl.ds(there, piece.shape[1])], sem)
    copy.start()
    copy.wait()


def place(ids, off, piece, result):
    return pl.pallas_call(
        functools.partial(place_kernel, off=off),
        grid_spec=pltpu.PrefetchScalarGridSpec(
            num_scalar_prefetch=1,
            grid=(1,),
            in_specs=[pl.BlockSpec(piece.shape, lambda i, ids: (0, 0)), ANY],
            out_specs=ANY,
            scratch_shapes=[pltpu.SemaphoreType.DMA],
        ),
        out_shape=jax.ShapeDtypeStruct(result.shape, result.dtype),
        input_output_aliases={2: 0},
        compiler_params=params(),
        cost_estimate=pl.CostEstimate(flops=0, bytes_accessed=0, transcendentals=0),
    )(ids, piece, result)


def adapter_kernel(core_ref, li_ref, down_ref, vg_ref, up_ref, keep_ref, give_ref, proj, pulled, *, factor):
    i = pl.program_id(0)
    step = li_ref.shape[1]
    rows = keep_ref.shape[1]
    blocks = pulled.shape[1] // rows
    per = keep_ref.shape[0] // blocks

    @pl.when(i == 0)
    def _():
        proj[...] = jnp.zeros_like(proj)
        pulled[...] = lax.dot_general(
            vg_ref[...], up_ref[...], (((1,), (1,)), ((), ())), preferred_element_type=f32
        ).astype(bf16)

    li = li_ref[...]
    proj[...] += lax.dot_general(
        li, down_ref[...], (((1,), (1,)), ((), ())), preferred_element_type=f32
    )
    part = factor * lax.dot_general(
        pulled[...], li, (((0,), (0,)), ((), ())), preferred_element_type=f32
    )
    mine = i // per == core_ref[0]

    def put(ref):
        for b in range(blocks):
            ref[b * per + i % per, :, :step] = part[b * rows : (b + 1) * rows]

    pl.when(mine)(lambda: put(keep_ref))
    pl.when(jnp.logical_not(mine))(lambda: put(give_ref))

    @pl.when(i == pl.num_programs(0) - 1)
    def _():
        up = factor * lax.dot_general(
            proj[...].astype(bf16), vg_ref[...], (((0,), (0,)), ((), ())), preferred_element_type=f32
        )
        h = up.shape[1] // 2
        w = h // per
        first = core_ref[0] == 0
        mine = jnp.where(first, up[:, :h], up[:, h:])
        other = jnp.where(first, up[:, h:], up[:, :h])
        for b in range(blocks):
            for c in range(per):
                part = slice(b * rows, (b + 1) * rows), slice(c * w, (c + 1) * w)
                keep_ref[b * per + c, :, step:] = mine[part]
                give_ref[b * per + c, :, step:] = other[part]


def adapter_parts(core, li, down_t, vg, up, factor, blocks=4, step=1024):
    tokens, width = li.shape
    rank, features = up.shape
    per = width // step // 2
    out = jax.ShapeDtypeStruct((blocks * per, rank // blocks, step + features // 2 // per), f32)
    whole = lambda a: pl.BlockSpec(a.shape, lambda i, c: (0,) * len(a.shape))
    return pl.pallas_call(
        functools.partial(adapter_kernel, factor=factor),
        grid_spec=pltpu.PrefetchScalarGridSpec(
            num_scalar_prefetch=1,
            grid=(width // step,),
            in_specs=[
                pl.BlockSpec((tokens, step), lambda i, c: (0, i)),
                pl.BlockSpec((rank, step), lambda i, c: (0, i)),
                whole(vg),
                whole(up),
            ],
            out_specs=[whole(out), whole(out)],
            scratch_shapes=[pltpu.VMEM((tokens, rank), f32), pltpu.VMEM((tokens, rank), bf16)],
        ),
        out_shape=[out, out],
        compiler_params=params(),
        cost_estimate=pl.CostEstimate(
            flops=4 * tokens * width * rank, bytes_accessed=2 * tokens * width + 4 * rank * width, transcendentals=0
        ),
    )(core, li, down_t, vg, up)


def finish_kernel(core_ref, mine, other, down_ref, up_ref, *, blocks):
    i = pl.program_id(0)
    step = down_ref.shape[1]
    per = mine.shape[0] // blocks

    def put(ref):
        for b in range(blocks):
            block = ref[b * per + i % per]
            rows = block.shape[0]
            down_ref[b * rows : (b + 1) * rows, :] = block[:, :step]
            up_ref[b * rows : (b + 1) * rows, :] = block[:, step:]

    pl.when(i < per)(lambda: put(mine))
    pl.when(i >= per)(lambda: put(other))


def finish(core, mine, other, rank, features, blocks=4, step=1024):
    per = mine.shape[0] // blocks
    whole = lambda a: pl.BlockSpec(a.shape, lambda i, c: (0,) * len(a.shape))
    at = lambda i, c: jnp.where(i < per, c[0], 1 - c[0]) * per + i % per
    return pl.pallas_call(
        functools.partial(finish_kernel, blocks=blocks),
        grid_spec=pltpu.PrefetchScalarGridSpec(
            num_scalar_prefetch=1,
            grid=(2 * per,),
            in_specs=[whole(mine), whole(other)],
            out_specs=[
                pl.BlockSpec((rank, step), lambda i, c: (0, at(i, c))),
                pl.BlockSpec((rank, features // 2 // per), lambda i, c: (0, at(i, c))),
            ],
        ),
        out_shape=[
            jax.ShapeDtypeStruct((rank, 2 * per * step), f32),
            jax.ShapeDtypeStruct((rank, features), f32),
        ],
        compiler_params=params(),
        cost_estimate=pl.CostEstimate(flops=0, bytes_accessed=8 * mine.size, transcendentals=0),
    )(core, mine, other)


def local(layer_input, value_grad, base_weight_t, adapter_down, adapter_up):
    core, x_hi, z = (lax.axis_index(a) for a in ("core", "x_hi", "z"))
    plane = ("x_lo", "y")
    tokens, features = value_grad.shape
    rank = adapter_up.shape[0]
    factor = adapter_scale / math.sqrt(tokens * math.prod(SIZES))
    down_t = adapter_down.T
    ids = jnp.stack([core, x_hi])

    mine = lax.dynamic_slice_in_dim(base_weight_t, core * HALF, HALF, 1)
    give = lax.dynamic_slice_in_dim(base_weight_t, (1 - core) * HALF, HALF, 1)
    got = flip(give, "core", 1)
    rows = lambda a, b: jnp.where(core == 0, jnp.concatenate([a, b]), jnp.concatenate([b, a]))
    chip_rows = rows(mine[:, ZCOLS:], got[:, ZCOLS:])

    keep, give = adapter_parts(
        ids, after(layer_input, chip_rows), down_t, value_grad, adapter_up, factor
    )
    total = keep + flip(give, "core", 1)
    total = lax.all_to_all(total, plane, 0, 0, tiled=True).reshape(8, 2, *total.shape[1:]).sum(0)
    total = total + flip(total, "x_hi", 1)
    pick = lambda at: lax.dynamic_index_in_dim(total, at % 2, 0, False)
    total = pick(z) + flip(pick(z + 1), "z", 1)
    near = lax.all_gather(chip_rows, "z", axis=0, tiled=True)
    near = after(near, total)
    far = cross_x(near)
    strip = rows(mine[:, :ZCOLS], got[:, :ZCOLS])
    strips = after(jnp.stack([strip, cross_x(strip)]), near, total)
    weight_z = lax.all_gather(strips, "z", axis=0, tiled=False)

    total = total + flip(total, "z", 2)
    total = total + flip(total, "z", 4)
    both = flip(total, "z", 1)
    total = jnp.where(z % 2 == 0, jnp.stack([total, both]), jnp.stack([both, total]))
    grads = jnp.concatenate([value_grad, flip(value_grad, "core", 1)], 0)
    pulled = lax.dot_general(
        grads, adapter_up, (((1,), (1,)), ((), ())), preferred_element_type=f32
    ).astype(bf16)
    pulled = (adapter_scale * pulled).astype(bf16)
    half = lax.all_to_all(
        jnp.broadcast_to(total, (8, *total.shape)).reshape(16, *total.shape[1:]), plane, 0, 0, tiled=True
    )
    result, send_u = product(ids, ZCOLS, grads, pulled, down_t, [near, far], step=1024)
    half = after(half, send_u)
    result, send_z = product(ids, 0, grads, pulled, down_t, [weight_z], result, step=1024)
    result = place(ids, ZCOLS, flip(send_u, "core", 1), result)
    result = place(ids, 0, flip(send_z, "core", 1), result)
    down_grad_t, up_grad = finish(ids, half, flip(half, "core", 1), rank, features)
    return (result, down_grad_t.T, up_grad)


def solution(mesh):
    fine = Mesh(mesh.devices.reshape(SIZES), AXES)
    return jax.shard_map(
        local,
        mesh=fine,
        in_specs=(P(AXES, None), P(AXES, None), P(("x_hi", "z", "core"), None), P(), P()),
        out_specs=(P(AXES, None), P(), P()),
        check_vma=False,
    )
```

```python
import functools
import math

import jax
import jax.numpy as jnp
from jax import lax
from jax.experimental import pallas as pl
from jax.experimental.pallas import tpu as pltpu
from jax.sharding import Mesh
from jax.sharding import PartitionSpec as P

adapter_scale = 2.0
AXES = ("x_lo", "y", "x_hi", "z", "core")
SIZES = (2, 4, 2, 8, 2)
D = 8192
HALF = D // 2
UCOLS = 2048
ZCOLS = HALF - UCOLS
f32, bf16 = jnp.float32, jnp.bfloat16
ANY = pl.BlockSpec(memory_space=pl.ANY)


def shift(x, axis, k):
    n = SIZES[AXES.index(axis)]
    return lax.ppermute(x, axis, [(i, (i + k) % n) for i in range(n)])


def flip(x, axis, k):
    n = SIZES[AXES.index(axis)]
    return lax.ppermute(x, axis, [(i, i ^ k) for i in range(n)])


def cross_x(x):
    return lax.ppermute(x, ("x_lo", "x_hi"), [(0, 3), (3, 0), (1, 2), (2, 1)])


def after(x, *others):
    return lax.optimization_barrier((x, *others))[0]


def params(mib=32):
    return pltpu.CompilerParams(vmem_limit_bytes=mib * 2**20)


def product_kernel(at_ref, grads, pulled, down, *refs, paired):
    own_ref, other_ref = refs[-2:]
    half, step = grads.shape[1] // 2, own_ref.shape[1]
    total = jnp.dot(pulled[...], down[...], preferred_element_type=f32)
    for far in (0, 1):
        at = pl.ds(pl.multiple_of((at_ref[1] + far) % 2 * half, 128), half)
        rows = refs[0][:, far].reshape(half, step) if paired else refs[far][...]
        total += jnp.dot(grads[:, at], rows, preferred_element_type=f32)
    total = total.astype(bf16)
    rows = own_ref.shape[0]
    own_ref[...] = total[:rows]
    other_ref[...] = total[rows:]


def product(ids, off, grads, pulled, down_t, weights, result=None, first=0, step=512):
    tokens, n = grads.shape[0], weights[-1].shape[-1]
    whole = lambda a: pl.BlockSpec(a.shape, lambda i, at: (0,) * a.ndim)
    args = [grads, pulled, down_t, *weights] + ([] if result is None else [result])
    block = lambda i, ids: (0, ids[0] * (HALF // step) + off // step + i)
    weight_spec = lambda w: pl.BlockSpec(
        (*w.shape[:-1], step), lambda i, at: (0,) * (w.ndim - 1) + (i + (first // step if w.shape[-1] > n else 0),)
    )
    return pl.pallas_call(
        functools.partial(product_kernel, paired=len(weights) == 1),
        grid_spec=pltpu.PrefetchScalarGridSpec(
            num_scalar_prefetch=1,
            grid=(n // step,),
            in_specs=[
                whole(grads),
                whole(pulled),
                pl.BlockSpec((pulled.shape[1], step), block),
            ]
            + [weight_spec(w) for w in weights]
            + ([] if result is None else [ANY]),
            out_specs=[
                pl.BlockSpec((tokens // 2, step), block),
                pl.BlockSpec((tokens // 2, step), lambda i, at: (0, i)),
            ],
        ),
        out_shape=[
            jax.ShapeDtypeStruct((tokens // 2, D), bf16),
            jax.ShapeDtypeStruct((tokens // 2, n), bf16),
        ],
        input_output_aliases={} if result is None else {len(args): 0},
        compiler_params=params(56),
        cost_estimate=pl.CostEstimate(flops=0, bytes_accessed=0, transcendentals=0),
    )(ids, *args)


def place_kernel(piece, _, out, sem, *, off):
    there = pl.multiple_of((1 - lax.axis_index("core")) * HALF + off, 128)
    copy = pltpu.make_async_copy(piece, out.at[:, pl.ds(there, piece.shape[1])], sem)
    copy.start()
    copy.wait()


def place(off, piece, result):
    return pl.pallas_call(
        functools.partial(place_kernel, off=off),
        in_specs=[pl.BlockSpec(memory_space=pltpu.VMEM), ANY],
        out_specs=ANY,
        scratch_shapes=[pltpu.SemaphoreType.DMA],
        out_shape=jax.ShapeDtypeStruct(result.shape, result.dtype),
        input_output_aliases={1: 0},
        compiler_params=params(),
        cost_estimate=pl.CostEstimate(flops=0, bytes_accessed=0, transcendentals=0),
    )(piece, result)


def adapter_kernel(core_ref, li_ref, down_ref, vg_ref, up_ref, keep_ref, give_ref, proj, pulled, *, factor):
    i = pl.program_id(0)
    step = li_ref.shape[1]
    rows = keep_ref.shape[1]
    blocks = pulled.shape[1] // rows
    per = keep_ref.shape[0] // blocks

    @pl.when(i == 0)
    def _():
        proj[...] = jnp.zeros_like(proj)
        pulled[...] = lax.dot_general(
            vg_ref[...], up_ref[...], (((1,), (1,)), ((), ())), preferred_element_type=f32
        ).astype(bf16)

    li = li_ref[...]
    proj[...] += lax.dot_general(
        li, down_ref[...], (((1,), (1,)), ((), ())), preferred_element_type=f32
    )
    part = factor * lax.dot_general(
        pulled[...], li, (((0,), (0,)), ((), ())), preferred_element_type=f32
    )
    mine = i // per == core_ref[0]

    def put(ref):
        for b in range(blocks):
            ref[b * per + i % per, :, :step] = part[b * rows : (b + 1) * rows]

    pl.when(mine)(lambda: put(keep_ref))
    pl.when(jnp.logical_not(mine))(lambda: put(give_ref))

    @pl.when(i == pl.num_programs(0) - 1)
    def _():
        up = factor * lax.dot_general(
            proj[...].astype(bf16), vg_ref[...], (((0,), (0,)), ((), ())), preferred_element_type=f32
        )
        h = up.shape[1] // 2
        w = h // per
        first = core_ref[0] == 0
        mine = jnp.where(first, up[:, :h], up[:, h:])
        other = jnp.where(first, up[:, h:], up[:, :h])
        for b in range(blocks):
            for c in range(per):
                part = slice(b * rows, (b + 1) * rows), slice(c * w, (c + 1) * w)
                keep_ref[b * per + c, :, step:] = mine[part]
                give_ref[b * per + c, :, step:] = other[part]


def adapter_parts(core, li, down_t, vg, up, factor, blocks=4, step=1024):
    tokens, width = li.shape
    rank, features = up.shape
    per = width // step // 2
    out = jax.ShapeDtypeStruct((blocks * per, rank // blocks, step + features // 2 // per), f32)
    whole = lambda a: pl.BlockSpec(a.shape, lambda i, c: (0,) * len(a.shape))
    return pl.pallas_call(
        functools.partial(adapter_kernel, factor=factor),
        grid_spec=pltpu.PrefetchScalarGridSpec(
            num_scalar_prefetch=1,
            grid=(width // step,),
            in_specs=[
                pl.BlockSpec((tokens, step), lambda i, c: (0, i)),
                pl.BlockSpec((rank, step), lambda i, c: (0, i)),
                whole(vg),
                whole(up),
            ],
            out_specs=[whole(out), whole(out)],
            scratch_shapes=[pltpu.VMEM((tokens, rank), f32), pltpu.VMEM((tokens, rank), bf16)],
        ),
        out_shape=[out, out],
        compiler_params=params(),
        cost_estimate=pl.CostEstimate(
            flops=4 * tokens * width * rank, bytes_accessed=2 * tokens * width + 4 * rank * width, transcendentals=0
        ),
    )(core, li, down_t, vg, up)


def finish_kernel(piece, *refs, other, blocks):
    down, up, sems = refs[-3:]
    half = lax.axis_index("core")
    half = 1 - half if other else half
    per, rows = piece.shape[0] // blocks, piece.shape[1]
    step = down.shape[1] // 2 // per
    width = piece.shape[2] - step
    copies = []
    for part in range(piece.shape[0]):
        to = pl.ds(part // per * rows, rows)
        for at, (out, n, first) in enumerate(((down, step, 0), (up, width, step))):
            there = pl.ds(pl.multiple_of(half * (per * n) + part % per * n, 128), n)
            source = piece.at[part, :, pl.ds(first, n)]
            copies.append(pltpu.make_async_copy(source, out.at[to, there], sems.at[part, at]))
    for copy in copies:
        copy.start()
    for copy in copies:
        copy.wait()


def finish(piece, rank, features, before=(), blocks=4):
    return pl.pallas_call(
        functools.partial(finish_kernel, other=bool(before), blocks=blocks),
        in_specs=[pl.BlockSpec(memory_space=pltpu.VMEM)] + [ANY] * len(before),
        out_specs=[ANY, ANY],
        scratch_shapes=[pltpu.SemaphoreType.DMA((piece.shape[0], 2))],
        out_shape=[jax.ShapeDtypeStruct((rank, D), f32), jax.ShapeDtypeStruct((rank, features), f32)],
        input_output_aliases={1: 0, 2: 1} if before else {},
        compiler_params=params(),
        cost_estimate=pl.CostEstimate(flops=0, bytes_accessed=0, transcendentals=0),
    )(piece, *before)


def local(layer_input, value_grad, base_weight_t, adapter_down, adapter_up):
    core, x_hi, z = (lax.axis_index(a) for a in ("core", "x_hi", "z"))
    plane = ("x_lo", "y")
    tokens, features = value_grad.shape
    rank = adapter_up.shape[0]
    factor = adapter_scale / math.sqrt(tokens * math.prod(SIZES))
    down_t = adapter_down.T
    ids = jnp.stack([core, x_hi])

    mine = lax.dynamic_slice_in_dim(base_weight_t, core * HALF, HALF, 1)
    give = lax.dynamic_slice_in_dim(base_weight_t, (1 - core) * HALF, HALF, 1)
    got = flip(give, "core", 1)
    rows = lambda a, b: jnp.where(core == 0, jnp.concatenate([a, b]), jnp.concatenate([b, a]))
    chip_rows = rows(mine[:, ZCOLS:], got[:, ZCOLS:])

    keep, give = adapter_parts(
        ids, after(layer_input, chip_rows), down_t, value_grad, adapter_up, factor
    )
    total = keep + flip(give, "core", 1)
    total = lax.all_to_all(total, plane, 0, 0, tiled=True).reshape(8, 2, *total.shape[1:]).sum(0)
    total = total + flip(total, "x_hi", 1)
    pick = lambda at: lax.dynamic_index_in_dim(total, at % 2, 0, False)
    total = pick(z) + flip(pick(z + 1), "z", 1)
    near = lax.all_gather(chip_rows, "z", axis=0, tiled=True)
    near = after(near, total)
    far = cross_x(near)
    strip = rows(mine[:, :ZCOLS], got[:, :ZCOLS])
    strips = after(jnp.stack([strip, cross_x(strip)]), near, total)
    weight_z = lax.all_gather(strips, "z", axis=0, tiled=False)

    total = total + flip(total, "z", 2)
    total = total + flip(total, "z", 4)
    both = flip(total, "z", 1)
    total = jnp.where(z % 2 == 0, jnp.stack([total, both]), jnp.stack([both, total]))
    grads = jnp.concatenate([value_grad, flip(value_grad, "core", 1)], 0)
    pulled = lax.dot_general(
        grads, adapter_up, (((1,), (1,)), ((), ())), preferred_element_type=f32
    ).astype(bf16)
    pulled = (adapter_scale * pulled).astype(bf16)
    half = lax.all_to_all(
        jnp.broadcast_to(total, (8, *total.shape)).reshape(16, *total.shape[1:]), plane, 0, 0, tiled=True
    )
    result, send_u = product(ids, ZCOLS, grads, pulled, down_t, [near, far], step=1024)
    half = after(half, send_u)
    sums = finish(half, rank, features)
    result, send_z = product(ids, 0, after(grads, *sums), pulled, down_t, [weight_z], result, step=1024)
    result = place(ZCOLS, flip(send_u, "core", 1), result)
    down_grad_t, up_grad = finish(flip(half, "core", 1), rank, features, sums)
    result = place(0, flip(send_z, "core", 1), result)
    return (result, down_grad_t.T, up_grad)


def solution(mesh):
    fine = Mesh(mesh.devices.reshape(SIZES), AXES)
    return jax.shard_map(
        local,
        mesh=fine,
        in_specs=(P(AXES, None), P(AXES, None), P(("x_hi", "z", "core"), None), P(), P()),
        out_specs=(P(AXES, None), P(), P()),
        check_vma=False,
    )
```

```python
import functools
import math

import jax
import jax.numpy as jnp
from jax import lax
from jax.experimental import pallas as pl
from jax.experimental.pallas import tpu as pltpu
from jax.sharding import Mesh
from jax.sharding import PartitionSpec as P

adapter_scale = 2.0
AXES = ("x_lo", "y", "x_hi", "z", "core")
SIZES = (2, 4, 2, 8, 2)
D = 8192
HALF = D // 2
UCOLS = 2048
ZCOLS = HALF - UCOLS
f32, bf16 = jnp.float32, jnp.bfloat16
ANY = pl.BlockSpec(memory_space=pl.ANY)


def shift(x, axis, k):
    n = SIZES[AXES.index(axis)]
    return lax.ppermute(x, axis, [(i, (i + k) % n) for i in range(n)])


def flip(x, axis, k):
    n = SIZES[AXES.index(axis)]
    return lax.ppermute(x, axis, [(i, i ^ k) for i in range(n)])


def cross_x(x):
    return lax.ppermute(x, ("x_lo", "x_hi"), [(0, 3), (3, 0), (1, 2), (2, 1)])


def after(x, *others):
    return lax.optimization_barrier((x, *others))[0]


def params(mib=32):
    return pltpu.CompilerParams(vmem_limit_bytes=mib * 2**20)


def product_kernel(at_ref, grads, pulled, down, *refs, paired):
    own_ref, other_ref = refs[-2:]
    half, step = grads.shape[1] // 2, own_ref.shape[1]
    total = jnp.dot(pulled[...], down[...], preferred_element_type=f32)
    for far in (0, 1):
        at = pl.ds(pl.multiple_of((at_ref[1] + far) % 2 * half, 128), half)
        rows = refs[0][:, far].reshape(half, step) if paired else refs[far][...]
        total += jnp.dot(grads[:, at], rows, preferred_element_type=f32)
    total = total.astype(bf16)
    rows = own_ref.shape[0]
    own_ref[...] = total[:rows]
    other_ref[...] = total[rows:]


def product(ids, off, grads, pulled, down_t, weights, result=None, first=0, step=512):
    tokens, n = grads.shape[0], weights[-1].shape[-1]
    whole = lambda a: pl.BlockSpec(a.shape, lambda i, at: (0,) * a.ndim)
    args = [grads, pulled, down_t, *weights] + ([] if result is None else [result])
    block = lambda i, ids: (0, ids[0] * (HALF // step) + off // step + i)
    weight_spec = lambda w: pl.BlockSpec(
        (*w.shape[:-1], step), lambda i, at: (0,) * (w.ndim - 1) + (i + (first // step if w.shape[-1] > n else 0),)
    )
    return pl.pallas_call(
        functools.partial(product_kernel, paired=len(weights) == 1),
        grid_spec=pltpu.PrefetchScalarGridSpec(
            num_scalar_prefetch=1,
            grid=(n // step,),
            in_specs=[
                whole(grads),
                whole(pulled),
                pl.BlockSpec((pulled.shape[1], step), block),
            ]
            + [weight_spec(w) for w in weights]
            + ([] if result is None else [ANY]),
            out_specs=[
                pl.BlockSpec((tokens // 2, step), block),
                pl.BlockSpec((tokens // 2, step), lambda i, at: (0, i)),
            ],
        ),
        out_shape=[
            jax.ShapeDtypeStruct((tokens // 2, D), bf16),
            jax.ShapeDtypeStruct((tokens // 2, n), bf16),
        ],
        input_output_aliases={} if result is None else {len(args): 0},
        compiler_params=params(56),
        cost_estimate=pl.CostEstimate(flops=0, bytes_accessed=0, transcendentals=0),
    )(ids, *args)


def place_kernel(piece, _, out, sem, *, off):
    there = pl.multiple_of((1 - lax.axis_index("core")) * HALF + off, 128)
    copy = pltpu.make_async_copy(piece, out.at[:, pl.ds(there, piece.shape[1])], sem)
    copy.start()
    copy.wait()


def place(off, piece, result):
    return pl.pallas_call(
        functools.partial(place_kernel, off=off),
        in_specs=[pl.BlockSpec(memory_space=pltpu.VMEM), ANY],
        out_specs=ANY,
        scratch_shapes=[pltpu.SemaphoreType.DMA],
        out_shape=jax.ShapeDtypeStruct(result.shape, result.dtype),
        input_output_aliases={1: 0},
        compiler_params=params(),
        cost_estimate=pl.CostEstimate(flops=0, bytes_accessed=0, transcendentals=0),
    )(piece, result)


def adapter_kernel(core_ref, li_ref, down_ref, vg_ref, up_ref, keep_ref, give_ref, proj, pulled, *, factor):
    i = pl.program_id(0)
    step = li_ref.shape[1]
    rows = keep_ref.shape[1]
    blocks = pulled.shape[1] // rows
    per = keep_ref.shape[0] // blocks

    @pl.when(i == 0)
    def _():
        proj[...] = jnp.zeros_like(proj)
        pulled[...] = lax.dot_general(
            vg_ref[...], up_ref[...], (((1,), (1,)), ((), ())), preferred_element_type=f32
        ).astype(bf16)

    li = li_ref[...]
    proj[...] += lax.dot_general(
        li, down_ref[...], (((1,), (1,)), ((), ())), preferred_element_type=f32
    )
    part = factor * lax.dot_general(
        pulled[...], li, (((0,), (0,)), ((), ())), preferred_element_type=f32
    )
    mine = i // per == core_ref[0]

    def put(ref):
        for b in range(blocks):
            ref[b * per + i % per, :, :step] = part[b * rows : (b + 1) * rows]

    pl.when(mine)(lambda: put(keep_ref))
    pl.when(jnp.logical_not(mine))(lambda: put(give_ref))

    @pl.when(i == pl.num_programs(0) - 1)
    def _():
        up = factor * lax.dot_general(
            proj[...].astype(bf16), vg_ref[...], (((0,), (0,)), ((), ())), preferred_element_type=f32
        )
        h = up.shape[1] // 2
        w = h // per
        first = core_ref[0] == 0
        mine = jnp.where(first, up[:, :h], up[:, h:])
        other = jnp.where(first, up[:, h:], up[:, :h])
        for b in range(blocks):
            for c in range(per):
                part = slice(b * rows, (b + 1) * rows), slice(c * w, (c + 1) * w)
                keep_ref[b * per + c, :, step:] = mine[part]
                give_ref[b * per + c, :, step:] = other[part]


def adapter_parts(core, li, down_t, vg, up, factor, blocks=4, step=1024):
    tokens, width = li.shape
    rank, features = up.shape
    per = width // step // 2
    out = jax.ShapeDtypeStruct((blocks * per, rank // blocks, step + features // 2 // per), f32)
    whole = lambda a: pl.BlockSpec(a.shape, lambda i, c: (0,) * len(a.shape))
    return pl.pallas_call(
        functools.partial(adapter_kernel, factor=factor),
        grid_spec=pltpu.PrefetchScalarGridSpec(
            num_scalar_prefetch=1,
            grid=(width // step,),
            in_specs=[
                pl.BlockSpec((tokens, step), lambda i, c: (0, i)),
                pl.BlockSpec((rank, step), lambda i, c: (0, i)),
                whole(vg),
                whole(up),
            ],
            out_specs=[whole(out), whole(out)],
            scratch_shapes=[pltpu.VMEM((tokens, rank), f32), pltpu.VMEM((tokens, rank), bf16)],
        ),
        out_shape=[out, out],
        compiler_params=params(),
        cost_estimate=pl.CostEstimate(
            flops=4 * tokens * width * rank, bytes_accessed=2 * tokens * width + 4 * rank * width, transcendentals=0
        ),
    )(core, li, down_t, vg, up)


def finish_kernel(piece, *refs, other, blocks):
    down, up, sems = refs[-3:]
    half = lax.axis_index("core")
    half = 1 - half if other else half
    per, rows = piece.shape[0] // blocks, piece.shape[1]
    step = down.shape[1] // 2 // per
    width = piece.shape[2] - step
    copies = []
    for part in range(piece.shape[0]):
        to = pl.ds(part // per * rows, rows)
        for at, (out, n, first) in enumerate(((down, step, 0), (up, width, step))):
            there = pl.ds(pl.multiple_of(half * (per * n) + part % per * n, 128), n)
            source = piece.at[part, :, pl.ds(first, n)]
            copies.append(pltpu.make_async_copy(source, out.at[to, there], sems.at[part, at]))
    for copy in copies:
        copy.start()
    for copy in copies:
        copy.wait()


def finish(piece, rank, features, before=(), blocks=4):
    return pl.pallas_call(
        functools.partial(finish_kernel, other=bool(before), blocks=blocks),
        in_specs=[pl.BlockSpec(memory_space=pltpu.VMEM)] + [ANY] * len(before),
        out_specs=[ANY, ANY],
        scratch_shapes=[pltpu.SemaphoreType.DMA((piece.shape[0], 2))],
        out_shape=[jax.ShapeDtypeStruct((rank, D), f32), jax.ShapeDtypeStruct((rank, features), f32)],
        input_output_aliases={1: 0, 2: 1} if before else {},
        compiler_params=params(),
        cost_estimate=pl.CostEstimate(flops=0, bytes_accessed=0, transcendentals=0),
    )(piece, *before)


def local(layer_input, value_grad, base_weight_t, adapter_down, adapter_up):
    core, x_hi, z = (lax.axis_index(a) for a in ("core", "x_hi", "z"))
    plane = ("x_lo", "y")
    tokens, features = value_grad.shape
    rank = adapter_up.shape[0]
    factor = adapter_scale / math.sqrt(tokens * math.prod(SIZES))
    down_t = adapter_down.T
    ids = jnp.stack([core, x_hi])

    mine = lax.dynamic_slice_in_dim(base_weight_t, core * HALF, HALF, 1)
    give = lax.dynamic_slice_in_dim(base_weight_t, (1 - core) * HALF, HALF, 1)
    got = flip(give, "core", 1)
    rows = lambda a, b: jnp.where(core == 0, jnp.concatenate([a, b]), jnp.concatenate([b, a]))
    chip_rows = rows(mine[:, ZCOLS:], got[:, ZCOLS:])

    keep, give = adapter_parts(
        ids, after(layer_input, chip_rows), down_t, value_grad, adapter_up, factor
    )
    total = keep + flip(give, "core", 1)
    total = lax.all_to_all(total, plane, 0, 0, tiled=True).reshape(8, 2, *total.shape[1:]).sum(0)
    pick = lambda at: lax.dynamic_index_in_dim(total, at % 2, 0, False)
    total = pick(z) + flip(pick(z + 1), "z", 1)
    total = total + flip(total, "x_hi", 1)
    near = lax.all_gather(chip_rows, "z", axis=0, tiled=True)
    near = after(near, total)
    far = cross_x(near)
    strip = rows(mine[:, :ZCOLS], got[:, :ZCOLS])
    strips = after(jnp.stack([strip, cross_x(strip)]), near, total)
    weight_z = lax.all_gather(strips, "z", axis=0, tiled=False)

    total = total + flip(total, "z", 2)
    total = total + flip(total, "z", 4)
    both = flip(total, "z", 1)
    total = jnp.where(z % 2 == 0, jnp.stack([total, both]), jnp.stack([both, total]))
    grads = jnp.concatenate([value_grad, flip(value_grad, "core", 1)], 0)
    pulled = lax.dot_general(
        grads, adapter_up, (((1,), (1,)), ((), ())), preferred_element_type=f32
    ).astype(bf16)
    pulled = (adapter_scale * pulled).astype(bf16)
    half = lax.all_to_all(
        jnp.broadcast_to(total, (8, *total.shape)).reshape(16, *total.shape[1:]), plane, 0, 0, tiled=True
    )
    result, send_u = product(ids, ZCOLS, grads, pulled, down_t, [near, far], step=1024)
    half = after(half, send_u)
    sums = finish(half, rank, features)
    result, send_z = product(ids, 0, after(grads, *sums), pulled, down_t, [weight_z], result, step=1024)
    result = place(ZCOLS, flip(send_u, "core", 1), result)
    down_grad_t, up_grad = finish(flip(half, "core", 1), rank, features, sums)
    result = place(0, flip(send_z, "core", 1), result)
    return (result, down_grad_t.T, up_grad)


def solution(mesh):
    fine = Mesh(mesh.devices.reshape(SIZES), AXES)
    return jax.shard_map(
        local,
        mesh=fine,
        in_specs=(P(AXES, None), P(AXES, None), P(("x_hi", "z", "core"), None), P(), P()),
        out_specs=(P(AXES, None), P(), P()),
        check_vma=False,
    )
```
